32 devices in a mesh: groups: 2 (over y), seq: 4 (over z), ffn: 2 (over x), row: 2 (over core).
Axes of the slice: x: 2, y: 2, z: 4, core: 2. Of those that a mesh axis runs over, the one named last changes fastest.
Arguments:
- hidden: bfloat16 [4, 2048, 14336], P(('groups', 'row'), 'seq', 'ffn'), parts along dimension 0, may hold values from -6 to 6
- out_grads: bfloat16 [4, 2048, 4096], P(('groups', 'row'), 'seq', 'ffn'), parts along dimension 0, may hold values from -6 to 6
- proj_in: bfloat16 [14336, 64], P('ffn'), may hold values from -0.046875 to 0.046875
- proj_out: bfloat16 [4096, 64], P('ffn'), may hold values from -0.09375 to 0.09375
- doc_lengths: int32 [4, 16], P(('groups', 'row')), parts along dimension 0, may hold values from 1 to 1024, 2048 in all within a row
Outputs:
- doc_grads: float32 [4, 16, 4096], P(('groups', 'row'), 'seq', 'ffn'), parts along dimension 0
- gram: float32 [8192, 4096], P(('groups', 'seq'), 'ffn'), parts along dimension 0
The draws below stay inside these ranges and needn't reach their ends.
There are 2 independent parts, one for each index of `groups`. The reference program is written for one: setup_inputs(seed, part) draws one part's arguments, and reference() takes and returns one part's arrays. A program takes and returns all parts, laid end to end along the dimension named above; an argument that names none is the same for every part. Nothing has to cross between parts.
Inputs may be any that keep to these rules, and one draw needn't show every extreme that they name: `doc_lengths`: the lengths of each packed row sum to 2048, and the longest of each row is 1024.
All inputs are finite; a program needn't handle non-finite values.
Results may differ from the reference program's by a relative error of at most 0.0003.
Values sent between devices are 32-bit elements; how exact they have to be, the bound alone decides.
A program may use at most 128 MiB of HBM per device.

```python
import math
import jax
import jax.numpy as jnp
import numpy as np
from jax import lax

D = 4096
FF = 14336
RANK = 64
SEQ_LEN = 2048
DOCS_ROW = 16
MOST_DOC = 1024
ROWS = 2


def steps_of(key, shape, split, low, largest):
    def one(axis_at, parts):
        heights = jax.random.uniform(jax.random.fold_in(jax.random.fold_in(key, 6), axis_at), (parts,), jnp.float32, low / len(split), largest / len(split))
        return jnp.repeat(jnp.exp(heights), shape[axis_at] // parts).reshape((-1,) + (1,) * (len(shape) - axis_at - 1))

    level = one(*split[0])
    for cut in split[1:]:
        level = level * one(*cut)
    return level


def profile(count, total, bound, slope):
    portions = [(1 << 20) // math.isqrt(standing ** slope) + 1 for standing in range(2, count + 1)]
    spare, given = total - bound - (count - 1), [1] * (count - 1)
    while spare > 0:
        movable = [i for i in range(count - 1) if given[i] < bound]
        whole, remaining = sum([portions[i] for i in movable]), spare
        for i in movable:
            more = min(bound - given[i], max(1, remaining * portions[i] // whole), spare)
            given[i] = given[i] + more
            spare = spare - more
    return np.array([bound] + given)


def uneven(key, count, total, reach, slope):
    if count == 2:
        one = jax.random.randint(key, (), max(1, total - reach), min(reach, total - 1) + 1)
        return jnp.stack([one, total - one])
    tallies = jnp.asarray(profile(count, total, reach, slope), jnp.int32)
    pairs = (count - 1) // 2
    donor, sink = tallies[1:1 + 2 * pairs:2], tallies[2:2 + 2 * pairs:2]
    room = jnp.minimum(donor - 1, reach - sink)
    shifted = jax.random.randint(jax.random.fold_in(key, 1), (pairs,), 0, 1 << 20) % (room + 1)
    tallies = tallies.at[1:1 + 2 * pairs:2].set(donor - shifted).at[2:2 + 2 * pairs:2].set(sink + shifted)
    return tallies[jax.random.permutation(jax.random.fold_in(key, 2), count)]


def normal_values(stream_key, shape, spread, most, pieces=(), kind=jnp.bfloat16):
    gain = steps_of(stream_key, shape, pieces, -0.22, 0.18) if pieces else 1.0
    entries = jax.random.normal(stream_key, shape, jnp.float32) * spread * gain
    return jnp.minimum(jnp.maximum(entries, -most), most).astype(kind)


def setup_inputs(seed: int = 0, part: int = 0) -> dict:
    seeds = jax.random.split(jax.random.key(seed), 6)
    own_keys = jax.random.split(jax.random.fold_in(seeds[5], part), 6)
    hidden = normal_values(own_keys[0], (ROWS, SEQ_LEN, FF), 1.0, 6.0, ((0, 2), (1, 4), (2, 2)))
    out_grads = normal_values(own_keys[1], (ROWS, SEQ_LEN, D), 1.0, 6.0, ((0, 2), (1, 4), (2, 2)))
    proj_in = normal_values(seeds[2], (FF, RANK), FF ** -0.5, 0.046875, ((0, 2),))
    proj_out = normal_values(seeds[3], (D, RANK), D ** -0.5, 0.09375, ((0, 2),))
    doc_lengths = jax.vmap(lambda own: uneven(own, DOCS_ROW, SEQ_LEN, MOST_DOC, 2))(jax.random.split(own_keys[4], ROWS)).reshape((ROWS, DOCS_ROW)).astype(jnp.int32)
    return {"hidden": hidden, "out_grads": out_grads, "proj_in": proj_in, "proj_out": proj_out, "doc_lengths": doc_lengths}


def doc_matrix(lengths_row, first, count):
    lengths_row = lengths_row.astype(jnp.int32)
    ends = jnp.cumsum(lengths_row).astype(jnp.int32)
    starts = (ends - lengths_row).astype(jnp.int32)
    position = (first + jnp.arange(count, dtype=jnp.int32)).astype(jnp.int32)
    inside = (position[None, :] >= starts[:, None]) & (position[None, :] < ends[:, None])
    return inside.astype(jnp.float32)

def reference(hidden, out_grads, proj_in, proj_out, doc_lengths):
    vectors = []
    for row_index in range(ROWS):
        input_proj = jnp.dot(hidden[row_index], proj_in, preferred_element_type=jnp.float32)
        output_proj = jnp.dot(out_grads[row_index], proj_out, preferred_element_type=jnp.float32)
        member = doc_matrix(doc_lengths[row_index], 0, SEQ_LEN)
        per_doc = jnp.einsum('dt,ti,tj->dij', member, output_proj, input_proj, precision=lax.Precision.HIGHEST)
        per_doc = per_doc.reshape(DOCS_ROW, RANK * RANK)
        scale = lax.rsqrt(doc_lengths[row_index].astype(jnp.float32))
        vectors.append(per_doc * scale[:, None])
    doc_grads = jnp.stack(vectors, axis=0)
    flat = doc_grads.reshape(ROWS * DOCS_ROW, RANK * RANK)
    gram = jnp.einsum('dk,dl->kl', flat, flat, precision=lax.Precision.HIGHEST) / (ROWS * DOCS_ROW)
    return (doc_grads, gram)
```

```python
import functools

import jax
import jax.numpy as jnp
from jax import lax
from jax.experimental import pallas as pl
from jax.experimental.pallas import tpu as pltpu
from jax.sharding import PartitionSpec as P

F32 = jnp.float32
BF16 = jnp.bfloat16
MESH = pl.DeviceIdType.MESH
CHUNKS = 4
NT = (((1,), (1,)), ((), ()))
TN = (((0,), (0,)), ((), ()))


def split(x):
    high = x.astype(BF16)
    return high, (x - high.astype(F32)).astype(BF16)


def remote(src, dst, send, recv, **where):
    return pltpu.make_async_remote_copy(
        src_ref=src, dst_ref=dst, send_sem=send, recv_sem=recv,
        device_id=where, device_id_type=MESH,
    )


def docs_kernel(
    S, F, R,
    hid, grads, p_in, p_out, lens,
    right_out, left_out, own_out,
    hbuf, gbuf, pib, pob, opart, ipart, orecv, irecv, a_hi, a_lo, rhs,
    pbuf, prec, vr, vl, vflat, lflat,
    ld_sem, o_send, o_recv, i_send, i_recv, p_send, p_recv,
    v_send, v_recv, b_send, b_recv, l_send, l_recv, m_send, m_recv,
):
    T = gbuf.shape[0]
    rank = pib.shape[1]
    docs = lens.shape[1]
    W = rank // F
    share = docs // S
    cols = W * rank
    trows = rank * rank // S
    q = S // F
    tc = T // CHUNKS
    s = lax.axis_index("seq")
    f = lax.axis_index("ffn")
    r = lax.axis_index("row")
    sib = 1 - r

    def load(src, dst, n):
        c = pltpu.make_async_copy(src, dst, ld_sem.at[n])
        c.start()
        return c

    lo_w = load(p_out, pob, 0)
    lo_x = load(grads.at[0], gbuf, 1)
    li_w = load(p_in, pib, 2)
    li_x = [
        load(hid.at[0, pl.ds(c * tc, tc)], hbuf.at[c], 3 + c) for c in range(CHUNKS)
    ]

    barrier = pltpu.get_barrier_semaphore()
    for ds in range(S):
        for df in range(F):
            if ds or df:
                pl.semaphore_signal(
                    barrier, inc=1,
                    device_id={"seq": lax.rem(s + ds, S), "ffn": lax.rem(f + df, F)},
                    device_id_type=MESH,
                )
    pl.semaphore_signal(barrier, inc=1, device_id={"row": sib}, device_id_type=MESH)

    row = lens[...].astype(F32)
    k_at = lax.broadcasted_iota(jnp.int32, (docs, docs), 0)
    m_at = lax.broadcasted_iota(jnp.int32, (docs, docs), 1)
    wide = jnp.broadcast_to(row, (docs, docs))
    ends = jnp.sum(jnp.where(m_at <= k_at, wide, 0.0), axis=1, keepdims=True)
    starts = jnp.sum(jnp.where(m_at < k_at, wide, 0.0), axis=1, keepdims=True)
    pos = (s * T + lax.broadcasted_iota(jnp.int32, (docs, T), 1)).astype(F32)
    inside = (pos >= starts) & (pos < ends)
    k_own = lax.broadcasted_iota(jnp.int32, (share, docs), 0) + s * share
    m_own = lax.broadcasted_iota(jnp.int32, (share, docs), 1)
    own_len = jnp.sum(
        jnp.where(m_own == k_own, jnp.broadcast_to(row, (share, docs)), 0.0),
        axis=1, keepdims=True,
    )
    own_scale = lax.rsqrt(own_len)

    waits = []
    lo_w.wait()
    lo_x.wait()
    o_here = jnp.dot(gbuf[...], pob[...], preferred_element_type=F32)
    o_t = o_here.T
    for g in range(F):
        opart[g] = o_t[g * W:(g + 1) * W]
    pl.semaphore_wait(barrier, S * F)
    o_copies = []
    for d in range(1, F):
        to = lax.rem(f + d, F)
        c = remote(opart.at[to], orecv.at[d], o_send.at[d], o_recv.at[d], ffn=to)
        c.start()
        o_copies.append(c)
    li_w.wait()
    i_copies = []
    for n in range(CHUNKS):
        li_x[n].wait()
        ipart[n] = jnp.dot(hbuf[n], pib[...], preferred_element_type=F32).T
        for d in range(1, F):
            c = remote(
                ipart.at[n], irecv.at[d, n], i_send.at[d, n], i_recv.at[d, n],
                ffn=lax.rem(f + d, F),
            )
            c.start()
            i_copies.append(c)

    for c in o_copies:
        c.wait_recv()
    o_sum = opart[f]
    for d in range(1, F):
        o_sum = o_sum + orecv[d]
    for i in range(W):
        masked = jnp.where(inside, o_sum[i:i + 1], 0.0)
        high, low = split(masked)
        a_hi[i * docs:(i + 1) * docs] = high
        a_lo[i * docs:(i + 1) * docs] = low
    for n in range(CHUNKS):
        i_sum = ipart[n]
        for d in range(1, F):
            i_copies[n * (F - 1) + d - 1].wait_recv()
            i_sum = i_sum + irecv[d, n]
        high, low = split(i_sum)
        at = slice(n * tc, (n + 1) * tc)
        rhs[0:rank, at] = high
        rhs[rank:2 * rank, at] = high
        rhs[2 * rank:3 * rank, at] = low
        rhs[3 * rank:4 * rank, at] = low
    big = lax.dot_general(a_hi[...], rhs[...], NT, preferred_element_type=F32)
    small = lax.dot_general(a_lo[...], rhs[:2 * rank], NT, preferred_element_type=F32)
    total = big[:, :2 * rank] + (big[:, 2 * rank:] + small)
    first = lax.broadcasted_iota(jnp.int32, (docs, 2 * rank), 1) < rank
    for p in range(W // 2):
        a = total[2 * p * docs:(2 * p + 1) * docs]
        b = total[(2 * p + 1) * docs:(2 * p + 2) * docs]
        tile = jnp.where(first, a, b)
        for g in range(S):
            pbuf[g, :, 2 * rank * p:2 * rank * (p + 1)] = tile[g * share:(g + 1) * share]

    p_copies = []
    for d in range(1, S):
        to = lax.rem(s + d, S)
        c = remote(pbuf.at[to], prec.at[d], p_send.at[d], p_recv.at[d], seq=to)
        c.start()
        p_copies.append(c)
    acc = pbuf[s]
    for d, c in enumerate(p_copies):
        c.wait_recv()
        acc = acc + prec[d + 1]
    own = acc * own_scale
    own_out[0] = own
    vr[r, s] = own

    v_copies = []
    for d in range(1, S):
        c = remote(
            vr.at[r, s], vr.at[r, s], v_send.at[d], v_recv.at[d],
            seq=lax.rem(s + d, S),
        )
        c.start()
        v_copies.append(c)
    l_copies = []
    for e in range(q):
        for d in range(1, F):
            c = remote(
                vr.at[r, s, :, pl.ds(e * trows, trows)], vl.at[r, s],
                l_send.at[e * (F - 1) + d - 1], l_recv.at[s],
                seq=q * f + e, ffn=lax.rem(f + d, F),
            )
            c.start()
            l_copies.append(c)
    b_copies = []
    for d in range(S):
        at = lax.rem(s + S - d, S)
        if d:
            v_copies[d - 1].wait_recv()
        c = remote(vr.at[r, at], vr.at[r, at], b_send.at[d], b_recv.at[d], row=sib)
        c.start()
        b_copies.append(c)

    need_left = f != s // q

    @pl.when(need_left)
    def _():
        for n in range(S):
            got = remote(
                vl.at[r, n], vl.at[r, n], m_send.at[n], l_recv.at[n], row=sib
            )
            got.wait_recv()
            remote(
                vl.at[r, n], vl.at[r, n], m_send.at[n], m_recv.at[n], row=sib
            ).start()

    for c in b_copies:
        c.wait_recv()
    half = R * S * share
    for a in range(R):
        for n in range(S):
            at = (a * S + n) * share
            vflat[at:at + share] = vr[a, n]
    high, low = split(vflat[...])
    right_out[0:half] = high
    right_out[half:2 * half] = low
    right_out[2 * half:3 * half] = high

    @pl.when(need_left)
    def _():
        for n in range(S):
            remote(
                vl.at[r, n], vl.at[r, n], m_send.at[n], m_recv.at[n], row=sib
            ).wait()
        for a in range(R):
            for n in range(S):
                at = (a * S + n) * share
                lflat[at:at + share] = vl[a, n]

    @pl.when(jnp.logical_not(need_left))
    def _():
        lflat[...] = vflat[:, pl.ds(pl.multiple_of(lax.rem(s, q) * trows, 128), trows)]

    high, low = split(lflat[...] * (1.0 / (R * docs)))
    left_out[0:half] = high
    left_out[half:2 * half] = high
    left_out[2 * half:3 * half] = low

    for c in o_copies + i_copies + p_copies + v_copies + l_copies + b_copies:
        c.wait_send()


def gram_kernel(left, right, own, gram, docs):
    gram[...] = lax.dot_general(left[...], right[...], TN, preferred_element_type=F32)

    @pl.when(pl.program_id(0) == 0)
    def _():
        docs[...] = own[...]


def local(hidden, out_grads, proj_in, proj_out, doc_lengths):
    S, F, R = (lax.axis_size(a) for a in ("seq", "ffn", "row"))
    T, H = hidden.shape[1:]
    D = out_grads.shape[2]
    rank = proj_in.shape[1]
    docs = doc_lengths.shape[1]
    W = rank // F
    share = docs // S
    cols = W * rank
    trows = rank * rank // S
    depth = R * docs
    tc = T // CHUNKS
    q = S // F
    dma = pltpu.SemaphoreType.DMA
    vmem = pl.BlockSpec(memory_space=pltpu.VMEM)
    hbm = pl.BlockSpec(memory_space=pl.ANY)
    right, left, own = pl.pallas_call(
        functools.partial(docs_kernel, S, F, R),
        out_shape=(
            jax.ShapeDtypeStruct((3 * depth, cols), BF16),
            jax.ShapeDtypeStruct((3 * depth, trows), BF16),
            jax.ShapeDtypeStruct((1, share, cols), F32),
        ),
        in_specs=[hbm, hbm, hbm, hbm, vmem],
        out_specs=(vmem, vmem, vmem),
        scratch_shapes=[
            pltpu.VMEM((CHUNKS, tc, H), BF16),
            pltpu.VMEM((T, D), BF16),
            pltpu.VMEM((H, rank), BF16),
            pltpu.VMEM((D, rank), BF16),
            pltpu.VMEM((F, W, T), F32),
            pltpu.VMEM((CHUNKS, rank, tc), F32),
            pltpu.VMEM((F, W, T), F32),
            pltpu.VMEM((F, CHUNKS, rank, tc), F32),
            pltpu.VMEM((W * docs, T), BF16),
            pltpu.VMEM((W * docs, T), BF16),
            pltpu.VMEM((4 * rank, T), BF16),
            pltpu.VMEM((S, share, cols), F32),
            pltpu.VMEM((S, share, cols), F32),
            pltpu.VMEM((R, S, share, cols), F32),
            pltpu.VMEM((R, S, share, trows), F32),
            pltpu.VMEM((depth, cols), F32),
            pltpu.VMEM((depth, trows), F32),
            dma((3 + CHUNKS,)),
            dma((F,)), dma((F,)),
            dma((F, CHUNKS)), dma((F, CHUNKS)),
            dma((S,)), dma((S,)),
            dma((S,)), dma((S,)),
            dma((S,)), dma((S,)),
            dma((q * F,)), dma((S,)),
            dma((S,)), dma((S,)),
        ],
        compiler_params=pltpu.CompilerParams(
            collective_id=0, has_side_effects=True, vmem_limit_bytes=48 << 20,
        ),
        name="docs",
    )(hidden, out_grads, proj_in, proj_out, doc_lengths)
    tm = min(128, trows)
    gram, doc_grads = pl.pallas_call(
        gram_kernel,
        grid=(trows // tm,),
        out_shape=(
            jax.ShapeDtypeStruct((trows, cols), F32),
            jax.ShapeDtypeStruct((1, share, cols), F32),
        ),
        in_specs=[
            pl.BlockSpec((3 * depth, tm), lambda i: (0, i)),
            pl.BlockSpec((3 * depth, cols), lambda i: (0, 0)),
            pl.BlockSpec((1, share, cols), lambda i: (0, 0, 0)),
        ],
        out_specs=(
            pl.BlockSpec((tm, cols), lambda i: (i, 0)),
            pl.BlockSpec((1, share, cols), lambda i: (0, 0, 0)),
        ),
        compiler_params=pltpu.CompilerParams(vmem_limit_bytes=32 << 20),
        name="gram",
    )(left, right, own)
    return (doc_grads, gram)


def solution(mesh):
    placed = (
        P(("groups", "row"), "seq", "ffn"),
        P(("groups", "row"), "seq", "ffn"),
        P("ffn", None),
        P("ffn", None),
        P(("groups", "row"), None),
    )
    return jax.shard_map(
        local,
        mesh=mesh,
        in_specs=placed,
        out_specs=(P(("groups", "row"), "seq", "ffn"), P(("groups", "seq"), "ffn")),
        check_vma=False,
    )
```

```python
import functools

import jax
import jax.numpy as jnp
from jax import lax
from jax.experimental import pallas as pl
from jax.experimental.pallas import tpu as pltpu
from jax.sharding import PartitionSpec as P

F32 = jnp.float32
BF16 = jnp.bfloat16
MESH = pl.DeviceIdType.MESH
CHUNKS = 4
NT = (((1,), (1,)), ((), ()))
TN = (((0,), (0,)), ((), ()))


def split(x):
    high = x.astype(BF16)
    return high, (x - high.astype(F32)).astype(BF16)


def remote(src, dst, send, recv, **where):
    return pltpu.make_async_remote_copy(
        src_ref=src, dst_ref=dst, send_sem=send, recv_sem=recv,
        device_id=where, device_id_type=MESH,
    )


def docs_kernel(
    S, F, R,
    hid, grads, p_in, p_out, lens,
    right_out, left_out, own_out,
    hbuf, gbuf, pib, pob, opart, ipart, orecv, irecv, a_hi, a_lo, rhs,
    pbuf, prec, vr, vl, vflat, lflat,
    ld_sem, o_send, o_recv, i_send, i_recv, p_send, p_recv,
    v_send, v_recv, b_send, b_recv, l_send, l_recv, m_send, m_recv,
):
    T = gbuf.shape[0]
    rank = pib.shape[0]
    docs = lens.shape[1]
    W = rank // F
    share = docs // S
    cols = W * rank
    trows = rank * rank // S
    q = S // F
    tc = T // CHUNKS
    s = lax.axis_index("seq")
    f = lax.axis_index("ffn")
    r = lax.axis_index("row")
    sib = 1 - r

    def load(src, dst, n):
        c = pltpu.make_async_copy(src, dst, ld_sem.at[n])
        c.start()
        return c

    lo_w = load(p_out, pob, 0)
    lo_x = load(grads.at[0], gbuf, 1)
    li_w = load(p_in, pib, 2)
    li_x = [
        load(hid.at[0, pl.ds(c * tc, tc)], hbuf.at[c], 3 + c) for c in range(CHUNKS)
    ]

    barrier = pltpu.get_barrier_semaphore()
    for ds in range(S):
        for df in range(F):
            if ds or df:
                pl.semaphore_signal(
                    barrier, inc=1,
                    device_id={"seq": lax.rem(s + ds, S), "ffn": lax.rem(f + df, F)},
                    device_id_type=MESH,
                )
    pl.semaphore_signal(barrier, inc=1, device_id={"row": sib}, device_id_type=MESH)

    row = lens[...].astype(F32)
    k_at = lax.broadcasted_iota(jnp.int32, (docs, docs), 0)
    m_at = lax.broadcasted_iota(jnp.int32, (docs, docs), 1)
    wide = jnp.broadcast_to(row, (docs, docs))
    ends = jnp.sum(jnp.where(m_at <= k_at, wide, 0.0), axis=1, keepdims=True)
    starts = jnp.sum(jnp.where(m_at < k_at, wide, 0.0), axis=1, keepdims=True)
    pos = (s * T + lax.broadcasted_iota(jnp.int32, (docs, T), 1)).astype(F32)
    inside = (pos >= starts) & (pos < ends)
    k_own = lax.broadcasted_iota(jnp.int32, (share, docs), 0) + s * share
    m_own = lax.broadcasted_iota(jnp.int32, (share, docs), 1)
    own_len = jnp.sum(
        jnp.where(m_own == k_own, jnp.broadcast_to(row, (share, docs)), 0.0),
        axis=1, keepdims=True,
    )
    own_scale = lax.rsqrt(own_len)

    waits = []
    lo_w.wait()
    lo_x.wait()
    o_here = lax.dot_general(gbuf[...], pob[...], NT, preferred_element_type=F32)
    o_t = o_here.T
    for g in range(F):
        opart[g] = o_t[g * W:(g + 1) * W]
    pl.semaphore_wait(barrier, S * F)
    o_copies = []
    for d in range(1, F):
        to = lax.rem(f + d, F)
        c = remote(opart.at[to], orecv.at[d], o_send.at[d], o_recv.at[d], ffn=to)
        c.start()
        o_copies.append(c)
    li_w.wait()
    i_copies = []
    for n in range(CHUNKS):
        li_x[n].wait()
        ipart[n] = lax.dot_general(hbuf[n], pib[...], NT, preferred_element_type=F32).T
        for d in range(1, F):
            c = remote(
                ipart.at[n], irecv.at[d, n], i_send.at[d, n], i_recv.at[d, n],
                ffn=lax.rem(f + d, F),
            )
            c.start()
            i_copies.append(c)

    for c in o_copies:
        c.wait_recv()
    o_sum = opart[f]
    for d in range(1, F):
        o_sum = o_sum + orecv[d]
    for i in range(W):
        masked = jnp.where(inside, o_sum[i:i + 1], 0.0)
        high, low = split(masked)
        a_hi[i * docs:(i + 1) * docs] = high
        a_lo[i * docs:(i + 1) * docs] = low
    for n in range(CHUNKS):
        i_sum = ipart[n]
        for d in range(1, F):
            i_copies[n * (F - 1) + d - 1].wait_recv()
            i_sum = i_sum + irecv[d, n]
        high, low = split(i_sum)
        at = slice(n * tc, (n + 1) * tc)
        rhs[0:rank, at] = high
        rhs[rank:2 * rank, at] = high
        rhs[2 * rank:3 * rank, at] = low
        rhs[3 * rank:4 * rank, at] = low
    first = lax.broadcasted_iota(jnp.int32, (docs, 2 * rank), 1) < rank
    pairs = W // (2 * q)
    p_copies = []
    for p in range(q):
        at = slice(2 * pairs * docs * p, 2 * pairs * docs * (p + 1))
        big = lax.dot_general(a_hi[at], rhs[...], NT, preferred_element_type=F32)
        small = lax.dot_general(a_lo[at], rhs[:2 * rank], NT, preferred_element_type=F32)
        total = big[:, :2 * rank] + (big[:, 2 * rank:] + small)
        for u in range(pairs):
            a = total[2 * u * docs:(2 * u + 1) * docs]
            b = total[(2 * u + 1) * docs:(2 * u + 2) * docs]
            tile = jnp.where(first, a, b)
            for g in range(S):
                pbuf[p, g, :, 2 * rank * u:2 * rank * (u + 1)] = tile[g * share:(g + 1) * share]
        for d in range(1, S):
            to = lax.rem(s + d, S)
            c = remote(pbuf.at[p, to], prec.at[p, d], p_send.at[p, d], p_recv.at[p, d], seq=to)
            c.start()
            p_copies.append(c)

    v_copies = []
    l_copies = []
    b_copies = []

    def relay(p, d):
        at = lax.rem(s + S - d, S)
        c = remote(
            vr.at[p, r, at], vr.at[p, r, at], b_send.at[p, d], b_recv.at[p, d], row=sib
        )
        c.start()
        b_copies.append(c)

    for p in range(q):
        acc = pbuf[p, s]
        for d in range(1, S):
            p_copies[p * (S - 1) + d - 1].wait_recv()
            acc = acc + prec[p, d]
        own = acc * own_scale
        own_out[0, :, p * trows:(p + 1) * trows] = own
        vr[p, r, s] = own
        for d in range(1, S):
            c = remote(
                vr.at[p, r, s], vr.at[p, r, s], v_send.at[p, d], v_recv.at[p, d],
                seq=lax.rem(s + d, S),
            )
            c.start()
            v_copies.append(c)
        for d in range(1, F):
            c = remote(
                vr.at[p, r, s], vl.at[r, s], l_send.at[p, d], l_recv.at[s],
                seq=q * f + p, ffn=lax.rem(f + d, F),
            )
            c.start()
            l_copies.append(c)
        relay(p, 0)
    for p in range(q):
        for d in range(1, S):
            v_copies[p * (S - 1) + d - 1].wait_recv()
            relay(p, d)

    need_left = f != s // q

    @pl.when(need_left)
    def _():
        for n in range(S):
            remote(
                vl.at[r, n], vl.at[r, n], m_send.at[n], l_recv.at[n], row=sib
            ).wait_recv()
            remote(
                vl.at[r, n], vl.at[r, n], m_send.at[n], m_recv.at[n], row=sib
            ).start()

    depth = R * S * share
    for p in range(q):
        for c in b_copies[p:p + 1] + b_copies[q + p * (S - 1):q + (p + 1) * (S - 1)]:
            c.wait_recv()
        for a in range(R):
            for n in range(S):
                at = (a * S + n) * share
                vflat[p, at:at + share] = vr[p, a, n]
        high, low = split(vflat[p])
        at = slice(p * trows, (p + 1) * trows)
        right_out[0:depth, at] = high
        right_out[depth:2 * depth, at] = low
        right_out[2 * depth:3 * depth, at] = high

    @pl.when(need_left)
    def _():
        for n in range(S):
            remote(
                vl.at[r, n], vl.at[r, n], m_send.at[n], m_recv.at[n], row=sib
            ).wait()
        for a in range(R):
            for n in range(S):
                at = (a * S + n) * share
                lflat[at:at + share] = vl[a, n]

    @pl.when(jnp.logical_not(need_left))
    def _():
        lflat[...] = vflat[lax.rem(s, q)]

    high, low = split(lflat[...] * (1.0 / (R * docs)))
    left_out[0:depth] = high
    left_out[depth:2 * depth] = high
    left_out[2 * depth:3 * depth] = low

    for c in o_copies + i_copies + p_copies + v_copies + l_copies + b_copies:
        c.wait_send()


def gram_kernel(left, right, own, gram, docs, tiles, sem, own_sem):
    own_copy = pltpu.make_async_copy(own, docs, own_sem)
    own_copy.start()
    rows = left[...].T
    copies = []
    for n in range(tiles.shape[0]):
        tm = tiles.shape[1]
        tiles[n] = jnp.dot(
            rows[n * tm:(n + 1) * tm], right[...], preferred_element_type=F32
        )
        c = pltpu.make_async_copy(tiles.at[n], gram.at[pl.ds(n * tm, tm)], sem.at[n])
        c.start()
        copies.append(c)
    for c in copies:
        c.wait()
    own_copy.wait()


def local(hidden, out_grads, proj_in, proj_out, doc_lengths):
    S, F, R = (lax.axis_size(a) for a in ("seq", "ffn", "row"))
    T, H = hidden.shape[1:]
    D = out_grads.shape[2]
    rank = proj_in.shape[1]
    docs = doc_lengths.shape[1]
    W = rank // F
    share = docs // S
    cols = W * rank
    trows = rank * rank // S
    depth = R * docs
    tc = T // CHUNKS
    q = S // F
    dma = pltpu.SemaphoreType.DMA
    vmem = pl.BlockSpec(memory_space=pltpu.VMEM)
    hbm = pl.BlockSpec(memory_space=pltpu.HBM)
    right, left, own = pl.pallas_call(
        functools.partial(docs_kernel, S, F, R),
        out_shape=(
            pltpu.VMEM((3 * depth, cols), BF16),
            pltpu.VMEM((3 * depth, trows), BF16),
            pltpu.VMEM((1, share, cols), F32),
        ),
        in_specs=[hbm, hbm, hbm, hbm, vmem],
        out_specs=(vmem, vmem, vmem),
        scratch_shapes=[
            pltpu.VMEM((CHUNKS, tc, H), BF16),
            pltpu.VMEM((T, D), BF16),
            pltpu.VMEM((rank, H), BF16),
            pltpu.VMEM((rank, D), BF16),
            pltpu.VMEM((F, W, T), F32),
            pltpu.VMEM((CHUNKS, rank, tc), F32),
            pltpu.VMEM((F, W, T), F32),
            pltpu.VMEM((F, CHUNKS, rank, tc), F32),
            pltpu.VMEM((W * docs, T), BF16),
            pltpu.VMEM((W * docs, T), BF16),
            pltpu.VMEM((4 * rank, T), BF16),
            pltpu.VMEM((q, S, share, trows), F32),
            pltpu.VMEM((q, S, share, trows), F32),
            pltpu.VMEM((q, R, S, share, trows), F32),
            pltpu.VMEM((R, S, share, trows), F32),
            pltpu.VMEM((q, depth, trows), F32),
            pltpu.VMEM((depth, trows), F32),
            dma((3 + CHUNKS,)),
            dma((F,)), dma((F,)),
            dma((F, CHUNKS)), dma((F, CHUNKS)),
            dma((q, S)), dma((q, S)),
            dma((q, S)), dma((q, S)),
            dma((q, S)), dma((q, S)),
            dma((q, F)), dma((S,)),
            dma((S,)), dma((S,)),
        ],
        compiler_params=pltpu.CompilerParams(
            collective_id=0, has_side_effects=True, vmem_limit_bytes=60 << 20,
        ),
        name="docs",
    )(hidden, out_grads, proj_in.T, proj_out.T, doc_lengths)
    tm = min(128, trows)
    gram, doc_grads = pl.pallas_call(
        gram_kernel,
        out_shape=(
            jax.ShapeDtypeStruct((trows, cols), F32),
            jax.ShapeDtypeStruct((1, share, cols), F32),
        ),
        in_specs=[vmem, vmem, vmem],
        out_specs=(hbm, hbm),
        scratch_shapes=[
            pltpu.VMEM((trows // tm, tm, cols), F32), dma((trows // tm,)), dma,
        ],
        compiler_params=pltpu.CompilerParams(vmem_limit_bytes=44 << 20),
        name="gram",
    )(left, right, own)
    return (doc_grads, gram)


def solution(mesh):
    placed = (
        P(("groups", "row"), "seq", "ffn"),
        P(("groups", "row"), "seq", "ffn"),
        P("ffn", None),
        P("ffn", None),
        P(("groups", "row"), None),
    )
    return jax.shard_map(
        local,
        mesh=mesh,
        in_specs=placed,
        out_specs=(P(("groups", "row"), "seq", "ffn"), P(("groups", "seq"), "ffn")),
        check_vma=False,
    )
```

```python
import functools

import jax
import jax.numpy as jnp
from jax import lax
from jax.experimental import pallas as pl
from jax.experimental.pallas import tpu as pltpu
from jax.sharding import PartitionSpec as P

F32 = jnp.float32
BF16 = jnp.bfloat16
MESH = pl.DeviceIdType.MESH
CHUNKS = 4
NT = (((1,), (1,)), ((), ()))
TN = (((0,), (0,)), ((), ()))


def split(x):
    high = x.astype(BF16)
    return high, (x - high.astype(F32)).astype(BF16)


def remote(src, dst, send, recv, **where):
    return pltpu.make_async_remote_copy(
        src_ref=src, dst_ref=dst, send_sem=send, recv_sem=recv,
        device_id=where, device_id_type=MESH,
    )


def docs_kernel(
    S, F, R,
    hid, grads, p_in, p_out, lens_hbm,
    right_out, left_out, own_out,
    lens, hbuf, gbuf, pib, pob, opart, ipart, orecv, irecv, a_hi, a_lo, rhs,
    pbuf, prec, vr, vl, vflat, lflat,
    ld_sem, o_send, o_recv, i_send, i_recv, p_send, p_recv,
    v_send, v_recv, b_send, b_recv, l_send, l_recv, m_send, m_recv,
):
    T = gbuf.shape[0]
    rank = pib.shape[0]
    docs = lens.shape[1]
    W = rank // F
    share = docs // S
    cols = W * rank
    trows = rank * rank // S
    q = S // F
    tc = T // CHUNKS
    s = lax.axis_index("seq")
    f = lax.axis_index("ffn")
    r = lax.axis_index("row")
    sib = 1 - r

    def load(src, dst, n):
        c = pltpu.make_async_copy(src, dst, ld_sem.at[n])
        c.start()
        return c

    lo_w = load(p_out, pob, 0)
    lo_x = load(grads.at[0], gbuf, 1)
    li_w = load(p_in, pib, 2)
    li_x = [
        load(hid.at[0, pl.ds(c * tc, tc)], hbuf.at[c], 3 + c) for c in range(CHUNKS)
    ]

    lens_x = load(lens_hbm, lens, 3 + CHUNKS)

    barrier = pltpu.get_barrier_semaphore()
    for ds in range(S):
        for df in range(F):
            if ds or df:
                pl.semaphore_signal(
                    barrier, inc=1,
                    device_id={"seq": lax.rem(s + ds, S), "ffn": lax.rem(f + df, F)},
                    device_id_type=MESH,
                )
    pl.semaphore_signal(barrier, inc=1, device_id={"row": sib}, device_id_type=MESH)

    lo_w.wait()
    lo_x.wait()
    o_here = lax.dot_general(gbuf[...], pob[...], NT, preferred_element_type=F32)
    o_t = o_here.T
    for g in range(F):
        opart[g] = o_t[g * W:(g + 1) * W]
    pl.semaphore_wait(barrier, S * F)
    o_copies = []
    for d in range(1, F):
        to = lax.rem(f + d, F)
        c = remote(opart.at[to], orecv.at[d], o_send.at[d], o_recv.at[d], ffn=to)
        c.start()
        o_copies.append(c)
    li_w.wait()
    i_copies = []
    for n in range(CHUNKS):
        li_x[n].wait()
        ipart[n] = lax.dot_general(hbuf[n], pib[...], NT, preferred_element_type=F32).T
        for d in range(1, F):
            c = remote(
                ipart.at[n], irecv.at[d, n], i_send.at[d, n], i_recv.at[d, n],
                ffn=lax.rem(f + d, F),
            )
            c.start()
            i_copies.append(c)

    lens_x.wait()
    row = lens[...].astype(F32)
    k_at = lax.broadcasted_iota(jnp.int32, (docs, docs), 0)
    m_at = lax.broadcasted_iota(jnp.int32, (docs, docs), 1)
    wide = jnp.broadcast_to(row, (docs, docs))
    ends = jnp.sum(jnp.where(m_at <= k_at, wide, 0.0), axis=1, keepdims=True)
    starts = jnp.sum(jnp.where(m_at < k_at, wide, 0.0), axis=1, keepdims=True)
    pos = (s * T + lax.broadcasted_iota(jnp.int32, (docs, T), 1)).astype(F32)
    inside = (pos >= starts) & (pos < ends)
    k_own = lax.broadcasted_iota(jnp.int32, (share, docs), 0) + s * share
    m_own = lax.broadcasted_iota(jnp.int32, (share, docs), 1)
    own_len = jnp.sum(
        jnp.where(m_own == k_own, jnp.broadcast_to(row, (share, docs)), 0.0),
        axis=1, keepdims=True,
    )
    own_scale = lax.rsqrt(own_len)

    for c in o_copies:
        c.wait_recv()
    o_sum = opart[f]
    for d in range(1, F):
        o_sum = o_sum + orecv[d]
    for i in range(W):
        masked = jnp.where(inside, o_sum[i:i + 1], 0.0)
        high, low = split(masked)
        a_hi[i * docs:(i + 1) * docs] = high
        a_lo[i * docs:(i + 1) * docs] = low
    for n in range(CHUNKS):
        i_sum = ipart[n]
        for d in range(1, F):
            i_copies[n * (F - 1) + d - 1].wait_recv()
            i_sum = i_sum + irecv[d, n]
        high, low = split(i_sum)
        at = slice(n * tc, (n + 1) * tc)
        rhs[0:rank, at] = high
        rhs[rank:2 * rank, at] = high
        rhs[2 * rank:3 * rank, at] = low
        rhs[3 * rank:4 * rank, at] = low
    first = lax.broadcasted_iota(jnp.int32, (docs, 2 * rank), 1) < rank
    pairs = W // (2 * q)
    p_copies = []
    for p in range(q):
        at = slice(2 * pairs * docs * p, 2 * pairs * docs * (p + 1))
        big = lax.dot_general(a_hi[at], rhs[...], NT, preferred_element_type=F32)
        small = lax.dot_general(a_lo[at], rhs[:2 * rank], NT, preferred_element_type=F32)
        total = big[:, :2 * rank] + (big[:, 2 * rank:] + small)
        for u in range(pairs):
            a = total[2 * u * docs:(2 * u + 1) * docs]
            b = total[(2 * u + 1) * docs:(2 * u + 2) * docs]
            tile = jnp.where(first, a, b)
            for g in range(S):
                pbuf[p, g, :, 2 * rank * u:2 * rank * (u + 1)] = tile[g * share:(g + 1) * share]
        for d in range(1, S):
            to = lax.rem(s + d, S)
            c = remote(pbuf.at[p, to], prec.at[p, d], p_send.at[p, d], p_recv.at[p, d], seq=to)
            c.start()
            p_copies.append(c)

    v_copies = []
    l_copies = []
    b_copies = []

    def relay(p, d):
        at = lax.rem(s + S - d, S)
        c = remote(
            vr.at[p, r, at], vr.at[p, r, at], b_send.at[p, d], b_recv.at[p, d], row=sib
        )
        c.start()
        b_copies.append(c)

    for p in range(q):
        acc = pbuf[p, s]
        for d in range(1, S):
            p_copies[p * (S - 1) + d - 1].wait_recv()
            acc = acc + prec[p, d]
        own = acc * own_scale
        own_out[0, :, p * trows:(p + 1) * trows] = own
        vr[p, r, s] = own
        for d in range(1, S):
            c = remote(
                vr.at[p, r, s], vr.at[p, r, s], v_send.at[p, d], v_recv.at[p, d],
                seq=lax.rem(s + d, S),
            )
            c.start()
            v_copies.append(c)
        for d in range(1, F):
            c = remote(
                vr.at[p, r, s], vl.at[r, s], l_send.at[p, d], l_recv.at[s],
                seq=q * f + p, ffn=lax.rem(f + d, F),
            )
            c.start()
            l_copies.append(c)
        relay(p, 0)
    for p in range(q):
        for d in range(1, S):
            v_copies[p * (S - 1) + d - 1].wait_recv()
            relay(p, d)

    need_left = f != s // q

    @pl.when(need_left)
    def _():
        for n in range(S):
            remote(
                vl.at[r, n], vl.at[r, n], m_send.at[n], l_recv.at[n], row=sib
            ).wait_recv()
            remote(
                vl.at[r, n], vl.at[r, n], m_send.at[n], m_recv.at[n], row=sib
            ).start()

    depth = R * S * share
    for p in range(q):
        for c in b_copies[p:p + 1] + b_copies[q + p * (S - 1):q + (p + 1) * (S - 1)]:
            c.wait_recv()
        for a in range(R):
            for n in range(S):
                at = (a * S + n) * share
                vflat[p, at:at + share] = vr[p, a, n]
        high, low = split(vflat[p])
        at = slice(p * trows, (p + 1) * trows)
        right_out[0:depth, at] = high
        right_out[depth:2 * depth, at] = low
        right_out[2 * depth:3 * depth, at] = high

    @pl.when(need_left)
    def _():
        for n in range(S):
            remote(
                vl.at[r, n], vl.at[r, n], m_send.at[n], m_recv.at[n], row=sib
            ).wait()
        for a in range(R):
            for n in range(S):
                at = (a * S + n) * share
                lflat[at:at + share] = vl[a, n]

    @pl.when(jnp.logical_not(need_left))
    def _():
        lflat[...] = vflat[lax.rem(s, q)]

    high, low = split(lflat[...] * (1.0 / (R * docs)))
    left_out[0:depth] = high
    left_out[depth:2 * depth] = high
    left_out[2 * depth:3 * depth] = low

    for c in o_copies + i_copies + p_copies + v_copies + l_copies + b_copies:
        c.wait_send()


def gram_kernel(left, right, own, gram, docs, tiles, sem, own_sem):
    own_copy = pltpu.make_async_copy(own, docs, own_sem)
    own_copy.start()
    rows = left[...].T
    copies = []
    for n in range(tiles.shape[0]):
        tm = tiles.shape[1]
        tiles[n] = jnp.dot(
            rows[n * tm:(n + 1) * tm], right[...], preferred_element_type=F32
        )
        c = pltpu.make_async_copy(tiles.at[n], gram.at[pl.ds(n * tm, tm)], sem.at[n])
        c.start()
        copies.append(c)
    for c in copies:
        c.wait()
    own_copy.wait()


def local(hidden, out_grads, proj_in, proj_out, doc_lengths):
    S, F, R = (lax.axis_size(a) for a in ("seq", "ffn", "row"))
    T, H = hidden.shape[1:]
    D = out_grads.shape[2]
    rank = proj_in.shape[1]
    docs = doc_lengths.shape[1]
    W = rank // F
    share = docs // S
    cols = W * rank
    trows = rank * rank // S
    depth = R * docs
    tc = T // CHUNKS
    q = S // F
    dma = pltpu.SemaphoreType.DMA
    vmem = pl.BlockSpec(memory_space=pltpu.VMEM)
    hbm = pl.BlockSpec(memory_space=pltpu.HBM)
    right, left, own = pl.pallas_call(
        functools.partial(docs_kernel, S, F, R),
        out_shape=(
            pltpu.VMEM((3 * depth, cols), BF16),
            pltpu.VMEM((3 * depth, trows), BF16),
            pltpu.VMEM((1, share, cols), F32),
        ),
        in_specs=[hbm] * 5,
        out_specs=(vmem, vmem, vmem),
        scratch_shapes=[
            pltpu.VMEM((1, docs), jnp.int32),
            pltpu.VMEM((CHUNKS, tc, H), BF16),
            pltpu.VMEM((T, D), BF16),
            pltpu.VMEM((rank, H), BF16),
            pltpu.VMEM((rank, D), BF16),
            pltpu.VMEM((F, W, T), F32),
            pltpu.VMEM((CHUNKS, rank, tc), F32),
            pltpu.VMEM((F, W, T), F32),
            pltpu.VMEM((F, CHUNKS, rank, tc), F32),
            pltpu.VMEM((W * docs, T), BF16),
            pltpu.VMEM((W * docs, T), BF16),
            pltpu.VMEM((4 * rank, T), BF16),
            pltpu.VMEM((q, S, share, trows), F32),
            pltpu.VMEM((q, S, share, trows), F32),
            pltpu.VMEM((q, R, S, share, trows), F32),
            pltpu.VMEM((R, S, share, trows), F32),
            pltpu.VMEM((q, depth, trows), F32),
            pltpu.VMEM((depth, trows), F32),
            dma((4 + CHUNKS,)),
            dma((F,)), dma((F,)),
            dma((F, CHUNKS)), dma((F, CHUNKS)),
            dma((q, S)), dma((q, S)),
            dma((q, S)), dma((q, S)),
            dma((q, S)), dma((q, S)),
            dma((q, F)), dma((S,)),
            dma((S,)), dma((S,)),
        ],
        compiler_params=pltpu.CompilerParams(
            collective_id=0, has_side_effects=True, vmem_limit_bytes=60 << 20,
        ),
        name="docs",
    )(hidden, out_grads, proj_in.T, proj_out.T, doc_lengths)
    tm = min(128, trows)
    gram, doc_grads = pl.pallas_call(
        gram_kernel,
        out_shape=(
            jax.ShapeDtypeStruct((trows, cols), F32),
            jax.ShapeDtypeStruct((1, share, cols), F32),
        ),
        in_specs=[vmem, vmem, vmem],
        out_specs=(hbm, hbm),
        scratch_shapes=[
            pltpu.VMEM((trows // tm, tm, cols), F32), dma((trows // tm,)), dma,
        ],
        compiler_params=pltpu.CompilerParams(vmem_limit_bytes=44 << 20),
        name="gram",
    )(left, right, own)
    return (doc_grads, gram)


def solution(mesh):
    placed = (
        P(("groups", "row"), "seq", "ffn"),
        P(("groups", "row"), "seq", "ffn"),
        P("ffn", None),
        P("ffn", None),
        P(("groups", "row"), None),
    )
    return jax.shard_map(
        local,
        mesh=mesh,
        in_specs=placed,
        out_specs=(P(("groups", "row"), "seq", "ffn"), P(("groups", "seq"), "ffn")),
        check_vma=False,
    )
```

```python
import functools

import jax
import jax.numpy as jnp
from jax import lax
from jax.experimental import pallas as pl
from jax.experimental.pallas import tpu as pltpu
from jax.sharding import PartitionSpec as P

F32 = jnp.float32
BF16 = jnp.bfloat16
MESH = pl.DeviceIdType.MESH
CHUNKS = 4
NT = (((1,), (1,)), ((), ()))
TN = (((0,), (0,)), ((), ()))


def ORDER(n):
    return sorted(range(1, n), key=lambda d: -min(d, n - d))


def split(x):
    high = x.astype(BF16)
    return high, (x - high.astype(F32)).astype(BF16)


def remote(src, dst, send, recv, **where):
    return pltpu.make_async_remote_copy(
        src_ref=src, dst_ref=dst, send_sem=send, recv_sem=recv,
        device_id=where, device_id_type=MESH,
    )


def docs_kernel(
    S, F, R,
    hid, grads, p_in, p_out, lens_hbm,
    right_out, left_out, own_out,
    lens, hbuf, gbuf, pib, pob, opart, ipart, orecv, irecv, a_hi, a_lo, rhs,
    begun, pbuf, prec, vr, vl, vflat, lflat,
    ld_sem, o_send, o_recv, i_send, i_recv, p_send, p_recv,
    v_send, v_recv, b_send, b_recv, l_send, l_recv, m_send, m_recv,
):
    T = gbuf.shape[0]
    rank = pib.shape[0]
    docs = lens.shape[1]
    W = rank // F
    share = docs // S
    cols = W * rank
    trows = rank * rank // S
    q = S // F
    tc = T // CHUNKS
    s = lax.axis_index("seq")
    f = lax.axis_index("ffn")
    r = lax.axis_index("row")
    sib = 1 - r

    def load(src, dst, n):
        c = pltpu.make_async_copy(src, dst, ld_sem.at[n])
        c.start()
        return c

    lo_w = load(p_out, pob, 0)
    lo_x = load(grads.at[0], gbuf, 1)
    li_w = load(p_in, pib, 2)
    li_x = [
        load(hid.at[0, pl.ds(c * tc, tc)], hbuf.at[c], 3 + c) for c in range(CHUNKS)
    ]

    lens_x = load(lens_hbm, lens, 3 + CHUNKS)

    barrier = pltpu.get_barrier_semaphore()
    for ds in range(S):
        for df in range(F):
            if ds or df:
                pl.semaphore_signal(
                    barrier, inc=1,
                    device_id={"seq": lax.rem(s + ds, S), "ffn": lax.rem(f + df, F)},
                    device_id_type=MESH,
                )
    pl.semaphore_signal(barrier, inc=1, device_id={"row": sib}, device_id_type=MESH)

    lo_w.wait()
    lo_x.wait()
    o_here = lax.dot_general(gbuf[...], pob[...], NT, preferred_element_type=F32)
    o_t = o_here.T
    for g in range(F):
        opart[g] = o_t[g * W:(g + 1) * W]
    pl.semaphore_wait(barrier, S * F)
    o_copies = []
    for d in range(1, F):
        to = lax.rem(f + d, F)
        c = remote(opart.at[to], orecv.at[d], o_send.at[d], o_recv.at[d], ffn=to)
        c.start()
        o_copies.append(c)
    li_w.wait()
    i_copies = []
    for n in range(CHUNKS):
        li_x[n].wait()
        ipart[n] = lax.dot_general(hbuf[n], pib[...], NT, preferred_element_type=F32).T
        for d in range(1, F):
            c = remote(
                ipart.at[n], irecv.at[d, n], i_send.at[d, n], i_recv.at[d, n],
                ffn=lax.rem(f + d, F),
            )
            c.start()
            i_copies.append(c)

    lens_x.wait()
    row = lens[...].astype(F32)
    k_at = lax.broadcasted_iota(jnp.int32, (docs, docs), 0)
    m_at = lax.broadcasted_iota(jnp.int32, (docs, docs), 1)
    wide = jnp.broadcast_to(row, (docs, docs))
    ends = jnp.sum(jnp.where(m_at <= k_at, wide, 0.0), axis=1, keepdims=True)
    starts = jnp.sum(jnp.where(m_at < k_at, wide, 0.0), axis=1, keepdims=True)
    pos = (s * T + lax.broadcasted_iota(jnp.int32, (docs, T), 1)).astype(F32)
    inside = (pos >= starts) & (pos < ends)
    k_own = lax.broadcasted_iota(jnp.int32, (share, docs), 0) + s * share
    m_own = lax.broadcasted_iota(jnp.int32, (share, docs), 1)
    own_len = jnp.sum(
        jnp.where(m_own == k_own, jnp.broadcast_to(row, (share, docs)), 0.0),
        axis=1, keepdims=True,
    )
    own_scale = lax.rsqrt(own_len)

    for c in o_copies:
        c.wait_recv()
    o_sum = opart[f]
    for d in range(1, F):
        o_sum = o_sum + orecv[d]
    for i in range(W):
        masked = jnp.where(inside, o_sum[i:i + 1], 0.0)
        high, low = split(masked)
        a_hi[i * docs:(i + 1) * docs] = high
        a_lo[i * docs:(i + 1) * docs] = low
    pairs = W // (2 * q)
    early = (CHUNKS - 1) * tc

    def product(p, lo, hi):
        at = slice(2 * pairs * docs * p, 2 * pairs * docs * (p + 1))
        big = lax.dot_general(
            a_hi[at, lo:hi], rhs[:, lo:hi], NT, preferred_element_type=F32
        )
        small = lax.dot_general(
            a_lo[at, lo:hi], rhs[:2 * rank, lo:hi], NT, preferred_element_type=F32
        )
        return big[:, :2 * rank] + (big[:, 2 * rank:] + small)

    for n in range(CHUNKS):
        if n == CHUNKS - 1:
            for p in range(q):
                begun[p] = product(p, 0, early)
        i_sum = ipart[n]
        for d in range(1, F):
            i_copies[n * (F - 1) + d - 1].wait_recv()
            i_sum = i_sum + irecv[d, n]
        high, low = split(i_sum)
        at = slice(n * tc, (n + 1) * tc)
        rhs[0:rank, at] = high
        rhs[rank:2 * rank, at] = high
        rhs[2 * rank:3 * rank, at] = low
        rhs[3 * rank:4 * rank, at] = low
    first = lax.broadcasted_iota(jnp.int32, (docs, 2 * rank), 1) < rank
    p_copies = []
    for p in range(q):
        total = begun[p] + product(p, early, T)
        for u in range(pairs):
            a = total[2 * u * docs:(2 * u + 1) * docs]
            b = total[(2 * u + 1) * docs:(2 * u + 2) * docs]
            tile = jnp.where(first, a, b)
            for g in range(S):
                pbuf[p, g, :, 2 * rank * u:2 * rank * (u + 1)] = tile[g * share:(g + 1) * share]
        for d in ORDER(S):
            to = lax.rem(s + d, S)
            c = remote(pbuf.at[p, to], prec.at[p, d], p_send.at[p, d], p_recv.at[p, d], seq=to)
            c.start()
            p_copies.append(c)

    v_copies = []
    l_copies = []
    b_copies = []

    def relay(p, d):
        at = lax.rem(s + S - d, S)
        c = remote(
            vr.at[p, r, at], vr.at[p, r, at], b_send.at[p, d], b_recv.at[p, d], row=sib
        )
        c.start()
        b_copies.append(c)

    for p in range(q):
        acc = pbuf[p, s]
        for d in range(1, S):
            p_copies[p * (S - 1) + ORDER(S).index(d)].wait_recv()
            acc = acc + prec[p, d]
        own = acc * own_scale
        own_out[0, :, p * trows:(p + 1) * trows] = own
        vr[p, r, s] = own
        for d in ORDER(S):
            c = remote(
                vr.at[p, r, s], vr.at[p, r, s], v_send.at[p, d], v_recv.at[p, d],
                seq=lax.rem(s + d, S),
            )
            c.start()
            v_copies.append(c)
        for d in range(1, F):
            c = remote(
                vr.at[p, r, s], vl.at[r, s], l_send.at[p, d], l_recv.at[s],
                seq=q * f + p, ffn=lax.rem(f + d, F),
            )
            c.start()
            l_copies.append(c)
        relay(p, 0)
    for p in range(q):
        for d in reversed(ORDER(S)):
            v_copies[p * (S - 1) + ORDER(S).index(d)].wait_recv()
            relay(p, d)

    need_left = f != s // q

    @pl.when(need_left)
    def _():
        for n in range(S):
            remote(
                vl.at[r, n], vl.at[r, n], m_send.at[n], l_recv.at[n], row=sib
            ).wait_recv()
            remote(
                vl.at[r, n], vl.at[r, n], m_send.at[n], m_recv.at[n], row=sib
            ).start()

    depth = R * S * share
    for p in range(q):
        for c in b_copies[p:p + 1] + b_copies[q + p * (S - 1):q + (p + 1) * (S - 1)]:
            c.wait_recv()
        for a in range(R):
            for n in range(S):
                at = (a * S + n) * share
                vflat[p, at:at + share] = vr[p, a, n]
        high, low = split(vflat[p])
        at = slice(p * trows, (p + 1) * trows)
        right_out[0:depth, at] = high
        right_out[depth:2 * depth, at] = low
        right_out[2 * depth:3 * depth, at] = high

    @pl.when(need_left)
    def _():
        for n in range(S):
            remote(
                vl.at[r, n], vl.at[r, n], m_send.at[n], m_recv.at[n], row=sib
            ).wait()
        for a in range(R):
            for n in range(S):
                at = (a * S + n) * share
                lflat[at:at + share] = vl[a, n]

    @pl.when(jnp.logical_not(need_left))
    def _():
        lflat[...] = vflat[lax.rem(s, q)]

    high, low = split(lflat[...] * (1.0 / (R * docs)))
    left_out[0:depth] = high
    left_out[depth:2 * depth] = high
    left_out[2 * depth:3 * depth] = low

    for c in o_copies + i_copies + p_copies + v_copies + l_copies + b_copies:
        c.wait_send()


def gram_kernel(left, right, own, gram, docs, tiles, sem, own_sem):
    own_copy = pltpu.make_async_copy(own, docs, own_sem)
    own_copy.start()
    rows = left[...].T
    copies = []
    for n in range(tiles.shape[0]):
        tm = tiles.shape[1]
        tiles[n] = jnp.dot(
            rows[n * tm:(n + 1) * tm], right[...], preferred_element_type=F32
        )
        c = pltpu.make_async_copy(tiles.at[n], gram.at[pl.ds(n * tm, tm)], sem.at[n])
        c.start()
        copies.append(c)
    for c in copies:
        c.wait()
    own_copy.wait()


def local(hidden, out_grads, proj_in, proj_out, doc_lengths):
    S, F, R = (lax.axis_size(a) for a in ("seq", "ffn", "row"))
    T, H = hidden.shape[1:]
    D = out_grads.shape[2]
    rank = proj_in.shape[1]
    docs = doc_lengths.shape[1]
    W = rank // F
    share = docs // S
    cols = W * rank
    trows = rank * rank // S
    depth = R * docs
    tc = T // CHUNKS
    q = S // F
    dma = pltpu.SemaphoreType.DMA
    vmem = pl.BlockSpec(memory_space=pltpu.VMEM)
    hbm = pl.BlockSpec(memory_space=pltpu.HBM)
    right, left, own = pl.pallas_call(
        functools.partial(docs_kernel, S, F, R),
        out_shape=(
            pltpu.VMEM((3 * depth, cols), BF16),
            pltpu.VMEM((3 * depth, trows), BF16),
            pltpu.VMEM((1, share, cols), F32),
        ),
        in_specs=[hbm] * 5,
        out_specs=(vmem, vmem, vmem),
        scratch_shapes=[
            pltpu.VMEM((1, docs), jnp.int32),
            pltpu.VMEM((CHUNKS, tc, H), BF16),
            pltpu.VMEM((T, D), BF16),
            pltpu.VMEM((rank, H), BF16),
            pltpu.VMEM((rank, D), BF16),
            pltpu.VMEM((F, W, T), F32),
            pltpu.VMEM((CHUNKS, rank, tc), F32),
            pltpu.VMEM((F, W, T), F32),
            pltpu.VMEM((F, CHUNKS, rank, tc), F32),
            pltpu.VMEM((W * docs, T), BF16),
            pltpu.VMEM((W * docs, T), BF16),
            pltpu.VMEM((4 * rank, T), BF16),
            pltpu.VMEM((q, W * docs // q, 2 * rank), F32),
            pltpu.VMEM((q, S, share, trows), F32),
            pltpu.VMEM((q, S, share, trows), F32),
            pltpu.VMEM((q, R, S, share, trows), F32),
            pltpu.VMEM((R, S, share, trows), F32),
            pltpu.VMEM((q, depth, trows), F32),
            pltpu.VMEM((depth, trows), F32),
            dma((4 + CHUNKS,)),
            dma((F,)), dma((F,)),
            dma((F, CHUNKS)), dma((F, CHUNKS)),
            dma((q, S)), dma((q, S)),
            dma((q, S)), dma((q, S)),
            dma((q, S)), dma((q, S)),
            dma((q, F)), dma((S,)),
            dma((S,)), dma((S,)),
        ],
        compiler_params=pltpu.CompilerParams(
            collective_id=0, has_side_effects=True, vmem_limit_bytes=60 << 20,
        ),
        name="docs",
    )(hidden, out_grads, proj_in.T, proj_out.T, doc_lengths)
    tm = min(128, trows)
    gram, doc_grads = pl.pallas_call(
        gram_kernel,
        out_shape=(
            jax.ShapeDtypeStruct((trows, cols), F32),
            jax.ShapeDtypeStruct((1, share, cols), F32),
        ),
        in_specs=[vmem, vmem, vmem],
        out_specs=(hbm, hbm),
        scratch_shapes=[
            pltpu.VMEM((trows // tm, tm, cols), F32), dma((trows // tm,)), dma,
        ],
        compiler_params=pltpu.CompilerParams(vmem_limit_bytes=44 << 20),
        name="gram",
    )(left, right, own)
    return (doc_grads, gram)


def solution(mesh):
    placed = (
        P(("groups", "row"), "seq", "ffn"),
        P(("groups", "row"), "seq", "ffn"),
        P("ffn", None),
        P("ffn", None),
        P(("groups", "row"), None),
    )
    return jax.shard_map(
        local,
        mesh=mesh,
        in_specs=placed,
        out_specs=(P(("groups", "row"), "seq", "ffn"), P(("groups", "seq"), "ffn")),
        check_vma=False,
    )
```
